256 devices in a mesh: qrow: 8 (over z), kcol: 32 (over y, x, core).
Axes of the slice: x: 4, y: 4, z: 8, core: 2. Of those that a mesh axis runs over, the one named last changes fastest.
Arguments:
- queries: bfloat16 [32768, 128], P(('qrow', 'kcol')), may hold values from -6 to 6
- keys: bfloat16 [32768, 128], P(('qrow', 'kcol')), may hold values from -6 to 6
- values: bfloat16 [32768, 128], P(('qrow', 'kcol')), may hold values from -6 to 6
- cotangent: bfloat16 [32768, 128], P(('qrow', 'kcol')), may hold values from -6 to 6
- order: int32 [1024], replicated, may hold values from 0 to 1023, each once
Outputs:
- output: float32 [32768, 128], P(('qrow', 'kcol'))
- query_grad: float32 [32768, 128], P(('qrow', 'kcol'))
- key_grad: float32 [32768, 128], P(('qrow', 'kcol'))
- value_grad: float32 [32768, 128], P(('qrow', 'kcol'))
The draws below stay inside these ranges and needn't reach their ends.
All inputs are finite; a program needn't handle non-finite values.
Results may differ from the reference program's by a relative error of at most 0.0057.
Values may be sent and summed in bfloat16 or wider, within the bound.
A program may use at most 64 MiB of HBM per device.

```python
import math
import jax
import jax.numpy as jnp
from jax import lax

D = 128
BLK = 32
SEQ = 32768
NBLK = 1024


def draw_queries(key, part):
    drawn = jax.random.normal(jax.random.fold_in(key, 21), (SEQ, D), jnp.float32)
    return jnp.clip(drawn, -6.0, 6.0).astype(jnp.bfloat16)


def draw_keys(key, part):
    drawn = jax.random.normal(jax.random.fold_in(key, 31), (SEQ, D), jnp.float32)
    return jnp.clip(drawn, -6.0, 6.0).astype(jnp.bfloat16)


def level_of(rng, extent, cuts, smallest, top_value):
    loudness = 1.0
    for axis_at, parts in cuts:
        draws = jax.random.uniform(jax.random.fold_in(jax.random.fold_in(rng, 6), axis_at), (parts,), jnp.float32, smallest / len(cuts), top_value / len(cuts))
        loudness = loudness * jnp.repeat(jnp.exp(draws), extent[axis_at] // parts).reshape((-1,) + (1,) * (len(extent) - 1 - axis_at))
    return loudness


def bell_draw(own_key, shape, spread, most, pieces=(), held_as=jnp.bfloat16):
    result = jax.random.normal(own_key, shape, jnp.float32) * spread
    if len(pieces) > 0:
        result = level_of(own_key, shape, pieces, -0.22, 0.18) * result
    return jnp.clip(result, min=-most, max=most).astype(held_as)


def setup_inputs(seed: int = 0) -> dict:
    streams_of = jax.random.split(jax.random.key(seed), 6)
    queries = draw_queries(jax.random.fold_in(streams_of[5], 71), 0)
    keys = draw_keys(jax.random.fold_in(streams_of[5], 71), 0)
    values = bell_draw(streams_of[2], (SEQ, D), 1.0, 6.0, ((0, 256),))
    cotangent = bell_draw(streams_of[3], (SEQ, D), 1.0, 6.0, ((0, 256),))
    order = jax.random.permutation(streams_of[4], NBLK).astype(jnp.int32)
    return {"queries": queries, "keys": keys, "values": values, "cotangent": cotangent, "order": order}


def positions(order):
    stored = jnp.arange(SEQ, dtype=jnp.int32)
    return (order[stored // BLK] * BLK + stored % BLK).astype(jnp.int32)

def reference(queries, keys, values, cotangent, order):
    placed = positions(order)
    score_scale = 1.0 / math.sqrt(D)
    block_rows = min(1024, SEQ)
    block_count = SEQ // block_rows
    query_blocks = queries.reshape(block_count, block_rows, D)
    grad_blocks = cotangent.reshape(block_count, block_rows, D)
    place_blocks = placed.reshape(block_count, block_rows)
    values_wide = values.astype(jnp.float32)

    def scores_of(query_block, place_block):
        scores = jnp.dot(query_block, keys.T, preferred_element_type=jnp.float32) * score_scale
        visible = placed[None, :] <= place_block[:, None]
        return (scores, visible)

    def forward(inputs):
        query_block, place_block = inputs
        scores, visible = scores_of(query_block, place_block)
        row_top = lax.optimization_barrier(jnp.max(jnp.where(visible, scores, -1e+30), axis=1))
        terms = jnp.where(visible, jnp.exp(scores - row_top[:, None]), 0.0)
        total = lax.optimization_barrier(jnp.sum(terms, axis=1))
        mixed = jnp.dot(terms, values_wide, preferred_element_type=jnp.float32, precision=lax.Precision.HIGHEST)
        return (mixed / total[:, None], row_top + jnp.log(total))
    outputs, log_totals = lax.map(forward, (query_blocks, place_blocks))
    output = outputs.reshape(SEQ, D)
    deltas = lax.optimization_barrier(jnp.sum(cotangent.astype(jnp.float32) * output, axis=1))
    deltas = deltas.reshape(block_count, block_rows)

    def backward(carry, inputs):
        key_sum, value_sum = carry
        query_block, grad_block, place_block, log_total, delta = inputs
        scores, visible = scores_of(query_block, place_block)
        probs = jnp.where(visible, jnp.exp(scores - log_total[:, None]), 0.0)
        value_sum = value_sum + jnp.dot(probs.astype(jnp.bfloat16).T, grad_block, preferred_element_type=jnp.float32)
        prob_grad = jnp.dot(grad_block, values.T, preferred_element_type=jnp.float32)
        score_grad = (probs * (prob_grad - delta[:, None])).astype(jnp.bfloat16)
        query_part = jnp.dot(score_grad, keys, preferred_element_type=jnp.float32) * score_scale
        key_sum = key_sum + jnp.dot(score_grad.T, query_block, preferred_element_type=jnp.float32) * score_scale
        return ((key_sum, value_sum), query_part)
    zeros = jnp.zeros((SEQ, D), jnp.float32)
    (key_sum, value_sum), query_parts = lax.scan(backward, (zeros, zeros), (query_blocks, grad_blocks, place_blocks, log_totals, deltas))
    growth = math.sqrt(SEQ * 0.5)
    query_grad = query_parts.reshape(SEQ, D) * growth
    key_grad = key_sum * growth
    value_grad = value_sum * growth
    return (output, query_grad, key_grad, value_grad)
```

```python
import math

import jax
import jax.numpy as jnp
from jax import lax
from jax.experimental import pallas as pl
from jax.experimental.pallas import tpu as pltpu
from jax.sharding import PartitionSpec as P

BLK = 32
MESH = pl.DeviceIdType.MESH
F32 = jnp.float32
BF16 = jnp.bfloat16
LOG2E = 1.4426950408889634


def dot(a, b, ca, cb):
    return lax.dot_general(a, b, (((ca,), (cb,)), ((), ())), preferred_element_type=F32)


def make_kernel(nz, ny, nx, nc, rows, width):
    nq = ny * nx
    nk = nz * nc
    seq = nq * nk * rows
    qn = nq * rows
    kn = nk * rows
    per = rows // BLK
    qw = nx * rows
    kw = nc * rows
    kb_count = kn // kw
    c2 = LOG2E / math.sqrt(width)
    grow = math.sqrt(rows * nq * nk * 0.5)
    side = grow / math.sqrt(width)

    def kernel(
        order_in, q_in, k_in, v_in, g_in, out_ref, dq_ref, dk_ref, dv_ref,
        order, qg, gg, kg, vg, qpos, kpos, scores, expo, dprob, dscore, stat, norm, stat_in,
        part, part_in, logs, logs_in, delta, delta_in, factor, mix, mix_in, dqs, dqs_in, own, core_out, core_in, z_out, z_in,
        load_sem, q_s, q_r, g_s, g_r, k_s, k_r, kf_s, kf_r, v_s, v_r, vf_s, vf_r,
        st_s, st_r, pt_s, pt_r, lg_s, lg_r, de_s, de_r, mx_s, mx_r, dq_s, dq_r, co_s, co_r, zz_s, zz_r,
    ):
        z = lax.axis_index("qrow")
        col = lax.axis_index("kcol")
        y = col // (nx * nc)
        x = (col // nc) % nx
        c = col % nc

        def wrap(a, n):
            return a % n if isinstance(a, int) else jnp.where(a >= n, a - n, a)

        across = [wrap(x + k, nx) * nc + c for k in range(nx)]
        down = [wrap(y + r, ny) * (nx * nc) for r in range(ny)]
        peers = [down[j // nx] + across[j % nx] for j in range(nq)]
        layers = [wrap(z + d, nz) for d in range(nz)]
        other = col + 1 - 2 * c if nc == 2 else col
        sibling = (z, other)

        def z_peer(d):
            return (layers[d] if isinstance(d, int) else wrap(z + d, nz), col)

        def xy_peer(j):
            return (z, peers[j])

        def back_row(r):
            return wrap(ny - r, ny)

        def back_col(k):
            return wrap(nx - k, nx)

        def neg(j):
            return back_row(j // nx) * nx + back_col(j % nx)

        def copy(src, dst, send, recv, target):
            return pltpu.make_async_remote_copy(
                src_ref=src, dst_ref=dst, send_sem=send, recv_sem=recv,
                device_id=target, device_id_type=MESH,
            )

        def span(j):
            return pl.ds(j * rows if isinstance(j, int) else pl.multiple_of(j * rows, rows), rows)

        barrier = pltpu.get_barrier_semaphore()

        for target in [xy_peer(j) for j in range(1, nq)] + [z_peer(d) for d in range(1, nz)] + [sibling]:
            pl.semaphore_signal(barrier, inc=1, device_id=target, device_id_type=MESH)
        order_load = pltpu.make_async_copy(order_in, order, load_sem.at[4])
        order_load.start()
        loads = []
        for i, (src, dst) in enumerate(((k_in, kg), (q_in, qg), (v_in, vg), (g_in, gg))):
            load = pltpu.make_async_copy(src, dst.at[pl.ds(0, rows)], load_sem.at[i])
            load.start()
            loads.append(load)
        for load in loads:
            load.wait()
        pl.semaphore_wait(barrier, nq - 1 + nz - 1 + 1)

        def z_copy(buf, s, r, d):
            return copy(buf.at[pl.ds(0, rows)], buf.at[span(nc * d)], s.at[0], r.at[d], z_peer(nz - d))

        def f_copy(buf, s, r, d):
            return copy(buf.at[span(nc * d)], buf.at[span(nc * d + 1)], s.at[0], r.at[0], sibling)

        def xy_copy(buf, s, r, j):
            return copy(buf.at[pl.ds(0, rows)], buf.at[span(j)], s.at[0], r.at[0], xy_peer(neg(j)))

        def settle(like, sem):
            pltpu.make_async_copy(like, like, sem).wait()

        def each(lo, hi, what):
            for i in range(lo, hi):
                what(i)

        each(1, nz, lambda d: z_copy(kg, k_s, k_r, d).start())
        each(1, nq, lambda j: xy_copy(qg, q_s, q_r, j).start())
        f_copy(kg, kf_s, kf_r, 0).start()
        each(1, nz, lambda d: z_copy(vg, v_s, v_r, d).start())
        each(1, nq, lambda j: xy_copy(gg, g_s, g_r, j).start())
        f_copy(vg, vf_s, vf_r, 0).start()

        lane = lax.broadcasted_iota(jnp.int32, (8, rows), 1)
        low = lax.broadcasted_iota(jnp.int32, (BLK, 128), 0)

        def place_q(j):
            first = (z * (nq * nc) + peers[j]) * per
            block = jnp.zeros((8, rows), jnp.int32)
            for b in range(per):
                block = jnp.where(lane // BLK == b, order[first + b], block)
            qpos[:, span(j)] = block * BLK + lane % BLK

        def place_k(j):
            first = (layers[j // nc] * (nq * nc) + (col, other)[j % nc]) * per
            for b in range(per):
                kpos[pl.ds(j * rows + b * BLK, BLK), :] = order[first + b] * BLK + low

        order_load.wait()
        each(0, nq, place_q)
        each(0, nk, place_k)

        def pass_on(buf, s, r, fs, fr):
            for i in range(1, nz):
                d = (i + 1) // 2 if i % 2 == 1 else nz - i // 2
                z_copy(buf, s, r, d).wait_recv()
                f_copy(buf, fs, fr, d).start()

        pass_on(kg, k_s, k_r, kf_s, kf_r)
        settle(kg.at[pl.ds(0, nz * rows)], kf_r.at[0])
        settle(qg.at[pl.ds(rows, (nq - 1) * rows)], q_r.at[0])

        def up_copy(src, into, s, r, row, k):
            j = row * nx + k
            m = back_row(row) * nx + back_col(k)
            if isinstance(row, int):
                target = peers[j]
            else:
                target = wrap(y + row, ny) * (nx * nc) + (across[k] if isinstance(k, int) else wrap(x + k, nx) * nc + c)
            return copy(src(j), into.at[m], s.at[0], r.at[0], (z, target))

        def top_copy(row, k):
            return up_copy(lambda j: stat.at[:, span(j)], stat_in, st_s, st_r, row, k)

        def mean_copy(row, k):
            return up_copy(lambda j: part.at[:, span(j)], part_in, pt_s, pt_r, row, k)

        def mix_copy(row, k):
            return up_copy(lambda j: mix.at[j], mix_in, mx_s, mx_r, row, k)

        def dq_copy(row, k):
            return up_copy(lambda j: dqs.at[j], dqs_in, dq_s, dq_r, row, k)

        def back_copy(buf, into, s, r, j):
            return copy(buf, into.at[j], s.at[0], r.at[0], xy_peer(neg(j)))

        def log_copy(j):
            return back_copy(logs, logs_in, lg_s, lg_r, j)

        def delta_copy(j):
            return back_copy(delta, delta_in, de_s, de_r, j)

        def send_row(maker, row):
            @pl.when(row > 0)
            def _():
                maker(row, 0).start()

            for k in range(1, nx):
                maker(row, k).start()

        def scores_step(i, carry):
            @pl.when(i == ny - 1)
            def _():
                pass_on(vg, v_s, v_r, vf_s, vf_r)

            r = wrap(i + 1, ny)
            qs = pl.ds(pl.multiple_of(r * qw, qw), qw)
            q = qg[qs, :]
            qp = qpos[:, qs]
            top = None
            for kb in range(kb_count):
                ks = slice(kb * kw, (kb + 1) * kw)
                s = dot(kg[ks, :], q, 1, 1) * c2
                kp = jnp.concatenate([kpos[ks, :]] * (qw // 128), axis=1)
                s = jnp.where(kp <= qp[0:1], s, -1e30)
                scores[ks, :] = s
                high = jnp.max(s.reshape(kw // 8, 8, qw), axis=0)
                top = high if top is None else jnp.maximum(top, high)
            top = jnp.maximum(jnp.max(top, axis=0, keepdims=True), -1e29)
            total = jnp.zeros((8, qw), F32)
            for kb in range(kb_count):
                ks = slice(kb * kw, (kb + 1) * kw)
                e = jnp.exp2(scores[ks, :] - top)
                total = total + jnp.sum(e.reshape(kw // 8, 8, qw), axis=0)
                expo[ks, qs] = e.astype(BF16)
            stat[0:1, qs] = top
            stat[1:2, qs] = jnp.sum(total, axis=0, keepdims=True)
            send_row(top_copy, r)
            return carry

        lax.fori_loop(0, ny, scores_step, 0)
        stat_in[0] = stat[:, 0:rows]

        settle(vg.at[pl.ds(0, nz * rows)], vf_r.at[0])
        settle(gg.at[pl.ds(rows, (nq - 1) * rows)], g_r.at[0])

        def dprob_step(i, carry):
            r = wrap(i + 1, ny)
            qs = pl.ds(pl.multiple_of(r * qw, qw), qw)
            g = gg[qs, :]
            acc = jnp.zeros((8, qw), F32)
            for kb in range(kb_count):
                ks = slice(kb * kw, (kb + 1) * kw)
                d = dot(vg[ks, :], g, 1, 1)
                dprob[ks, qs] = d
                acc = acc + jnp.sum((expo[ks, qs].astype(F32) * d).reshape(kw // 8, 8, qw), axis=0)
            part[:, qs] = acc
            send_row(mean_copy, r)
            return carry

        lax.fori_loop(0, ny - 1, dprob_step, 0)

        settle(stat_in.at[pl.ds(1, nq - 1)], st_r.at[0])
        tops = stat_in[:, 0, :]
        best = jnp.max(tops, axis=0, keepdims=True)
        scale = jnp.exp2(tops - best)
        total = jnp.sum(stat_in[:, 1, :] * scale, axis=0, keepdims=True)
        factor[...] = scale / total
        logs[...] = jnp.broadcast_to(best + jnp.log(total) * LOG2E, (8, rows))
        each(1, nq, lambda j: log_copy(j).start())
        logs_in[0] = logs[...]

        lax.fori_loop(ny - 1, ny, dprob_step, 0)
        part_in[0] = part[:, 0:rows]

        def mix_step(i, carry):
            r = wrap(i + 1, ny)
            qs = pl.ds(pl.multiple_of(r * qw, qw), qw)
            o = dot(vg[...], expo[:, qs], 0, 0).astype(BF16)
            for k in range(nx):
                mix[r * nx + k] = o[:, k * rows:(k + 1) * rows]
            return carry

        lax.fori_loop(0, ny - 1, mix_step, 0)

        settle(part_in.at[pl.ds(1, nq - 1)], pt_r.at[0])
        acc = jnp.zeros((8, rows), F32)
        for j in range(nq):
            acc = acc + part_in[j] * factor[j:j + 1, :]
        delta[...] = jnp.broadcast_to(jnp.sum(acc, axis=0, keepdims=True), (8, rows))
        each(1, nq, lambda j: delta_copy(j).start())
        delta_in[0] = delta[...]

        lax.fori_loop(ny - 1, ny, mix_step, 0)

        settle(logs_in.at[pl.ds(1, nq - 1)], lg_r.at[0])

        def spread_logs(j):
            norm[0:1, span(j)] = jnp.exp2(stat[0:1, span(j)] - logs_in[j, 0:1, :])

        each(0, nq, spread_logs)

        def core_copy(n, d):
            return copy(core_out.at[n, d], core_in.at[n, d], co_s.at[0], co_r.at[n, d], sibling)

        def zz_copy(n, d):
            return copy(
                z_out.at[n, d], z_in.at[n, nz - d], zz_s.at[0], zz_r.at[n], z_peer(d)
            )

        lag = 3

        def hand_on(n, d, value):
            own[n, d] = value[0:rows]
            core_out[n, d] = value[rows:].astype(BF16)
            core_copy(n, d).start()

        def to_owner(n, d):
            core_copy(n, d).wait_recv()
            z_out[n, d] = (own[n, d] + core_in[n, d].astype(F32)).astype(BF16)
            zz_copy(n, d).start()

        def send_mix(j):
            mix_copy(j // nx, j - j // nx * nx).start()

        qb = 512

        def values_step(i, carry):
            send_mix(i + 1)
            d = wrap(i + 1, nz)
            ks = pl.ds(pl.multiple_of(d * kw, kw), kw)
            dv = jnp.zeros((kw, width), F32)
            for b in range(qn // qb):
                qs = slice(b * qb, (b + 1) * qb)
                p = expo[ks, qs].astype(F32) * norm[0:1, qs]
                dv = dv + dot(p.astype(BF16), gg[qs, :], 1, 0)
            hand_on(0, d, dv)

            @pl.when(i >= lag)
            def _():
                to_owner(0, i - lag + 1)

            return carry

        lax.fori_loop(0, nz, values_step, 0)

        settle(delta_in.at[pl.ds(1, nq - 1)], de_r.at[0])

        def spread_delta(j):
            norm[1:2, span(j)] = delta_in[j, 0:1, :]

        each(0, nq, spread_delta)

        def keys_step(i, carry):
            @pl.when(i < nq - 1 - nz)
            def _():
                send_mix(i + 1 + nz)

            d = wrap(i + 1, nz)
            ks = pl.ds(pl.multiple_of(d * kw, kw), kw)
            dk = jnp.zeros((kw, width), F32)
            for b in range(qn // qb):
                qs = slice(b * qb, (b + 1) * qb)
                p = expo[ks, qs].astype(F32) * norm[0:1, qs]
                ds = (p * (dprob[ks, qs] - norm[1:2, qs])).astype(BF16)
                dscore[ks, qs] = ds
                dk = dk + dot(ds, qg[qs, :], 1, 0)
            hand_on(1, d, dk)

            @pl.when(i < lag - 1)
            def _():
                to_owner(0, i + nz - lag + 1)

            @pl.when(i >= lag)
            def _():
                to_owner(1, i - lag + 1)

            return carry

        lax.fori_loop(0, nz, keys_step, 0)

        def queries_step(i, carry):
            r = wrap(i + 1, ny)
            qs = pl.ds(pl.multiple_of(r * qw, qw), qw)
            o = dot(kg[...], dscore[:, qs], 0, 0)
            for k in range(nx):
                dqs[r * nx + k] = o[:, k * rows:(k + 1) * rows].astype(BF16)
            send_row(dq_copy, r)

            @pl.when(i < lag - 1)
            def _():
                to_owner(1, i + nz - lag + 1)

            return carry

        lax.fori_loop(0, ny, queries_step, 0)

        settle(mix_in.at[pl.ds(1, nq - 1)], mx_r.at[0])
        acc = mix[0].astype(F32) * factor[0:1, :]
        for j in range(1, nq):
            acc = acc + mix_in[j].astype(F32) * factor[j:j + 1, :]
        out_ref[...] = acc.T

        for n, ref, by in ((0, dv_ref, grow), (1, dk_ref, side)):
            core_copy(n, 0).wait_recv()
            settle(z_in.at[n, pl.ds(1, nz - 1)], zz_r.at[n])
            acc = own[n, 0] + core_in[n, 0].astype(F32)
            for d in range(1, nz):
                acc = acc + z_in[n, d].astype(F32)
            ref[...] = acc * by

        settle(dqs_in.at[pl.ds(1, nq - 1)], dq_r.at[0])
        acc = dqs[0].astype(F32)
        for j in range(1, nq):
            acc = acc + dqs_in[j].astype(F32)
        dq_ref[...] = acc.T * side

        for like, sem in (
            (qg.at[pl.ds(0, (nq - 1) * rows)], q_s), (gg.at[pl.ds(0, (nq - 1) * rows)], g_s),
            (kg.at[pl.ds(0, (nz - 1) * rows)], k_s), (vg.at[pl.ds(0, (nz - 1) * rows)], v_s),
            (kg.at[pl.ds(0, nz * rows)], kf_s), (vg.at[pl.ds(0, nz * rows)], vf_s),
            (stat_in.at[pl.ds(1, nq - 1)], st_s), (part_in.at[pl.ds(1, nq - 1)], pt_s),
            (logs_in.at[pl.ds(1, nq - 1)], lg_s), (delta_in.at[pl.ds(1, nq - 1)], de_s),
            (mix.at[pl.ds(1, nq - 1)], mx_s), (dqs.at[pl.ds(1, nq - 1)], dq_s),
            (core_out, co_s), (z_out.at[:, pl.ds(1, nz - 1)], zz_s),
        ):
            settle(like, sem.at[0])

    dma = pltpu.SemaphoreType.DMA
    scratch = [
        pltpu.SMEM((seq // BLK,), jnp.int32),
        pltpu.VMEM((qn, width), BF16), pltpu.VMEM((qn, width), BF16),
        pltpu.VMEM((kn, width), BF16), pltpu.VMEM((kn, width), BF16),
        pltpu.VMEM((8, qn), jnp.int32), pltpu.VMEM((kn, 128), jnp.int32),
        pltpu.VMEM((kn, qw), F32), pltpu.VMEM((kn, qn), BF16),
        pltpu.VMEM((kn, qn), F32), pltpu.VMEM((kn, qn), BF16),
        pltpu.VMEM((8, qn), F32), pltpu.VMEM((8, qn), F32), pltpu.VMEM((nq, 8, rows), F32),
        pltpu.VMEM((8, qn), F32), pltpu.VMEM((nq, 8, rows), F32),
        pltpu.VMEM((8, rows), F32), pltpu.VMEM((nq, 8, rows), F32),
        pltpu.VMEM((8, rows), F32), pltpu.VMEM((nq, 8, rows), F32),
        pltpu.VMEM((nq, rows), F32),
        pltpu.VMEM((nq, width, rows), BF16), pltpu.VMEM((nq, width, rows), BF16),
        pltpu.VMEM((nq, width, rows), BF16), pltpu.VMEM((nq, width, rows), BF16),
        pltpu.VMEM((2, nz, rows, width), F32),
        pltpu.VMEM((2, nz, rows, width), BF16), pltpu.VMEM((2, nz, rows, width), BF16),
        pltpu.VMEM((2, nz, rows, width), BF16), pltpu.VMEM((2, nz, rows, width), BF16),
        dma((5,)),
        dma((1,)), dma((1,)), dma((1,)), dma((1,)),
        dma((1,)), dma((nz,)), dma((1,)), dma((1,)),
        dma((1,)), dma((nz,)), dma((1,)), dma((1,)),
        dma((1,)), dma((1,)), dma((1,)), dma((1,)),
        dma((1,)), dma((1,)), dma((1,)), dma((1,)),
        dma((1,)), dma((1,)), dma((1,)), dma((1,)),
        dma((1,)), dma((2, nz)), dma((1,)), dma((2,)),
    ]
    vmem = pl.BlockSpec(memory_space=pltpu.VMEM)
    hbm = pl.BlockSpec(memory_space=pl.ANY)
    result = jax.ShapeDtypeStruct((rows, width), F32)
    return pl.pallas_call(
        kernel,
        name="banded_attention",
        out_shape=(result,) * 4,
        in_specs=[hbm] * 5,
        out_specs=(vmem,) * 4,
        scratch_shapes=scratch,
        compiler_params=pltpu.CompilerParams(
            collective_id=0, has_side_effects=True, vmem_limit_bytes=56 * 1024 * 1024
        ),
    )


def write_out(arrays, rows, width):
    def kernel(a, b, c, d, a_out, b_out, c_out, d_out):
        for source, target in ((a, a_out), (b, b_out), (c, c_out), (d, d_out)):
            target[...] = source[...]

    vmem = pl.BlockSpec(memory_space=pltpu.VMEM)
    return pl.pallas_call(
        kernel,
        name="write_out",
        out_shape=(jax.ShapeDtypeStruct((rows, width), F32),) * 4,
        in_specs=[vmem] * 4,
        out_specs=(vmem,) * 4,
        compiler_params=pltpu.CompilerParams(vmem_limit_bytes=56 * 1024 * 1024),
    )(*arrays)


def solution(mesh):
    nz = mesh.shape["qrow"]
    nc = 2
    nx = math.isqrt(mesh.shape["kcol"] // nc)
    ny = mesh.shape["kcol"] // (nc * nx)

    def body(queries, keys, values, cotangent, order):
        rows, width = queries.shape
        call = make_kernel(nz, ny, nx, nc, rows, width)
        return write_out(call(order, queries, keys, values, cotangent), rows, width)

    held = P(("qrow", "kcol"), None)
    return jax.shard_map(
        body,
        mesh=mesh,
        in_specs=(held, held, held, held, P()),
        out_specs=(held,) * 4,
        check_vma=False,
    )
```

```python
import math

import jax
import jax.numpy as jnp
from jax import lax
from jax.experimental import pallas as pl
from jax.experimental.pallas import tpu as pltpu
from jax.sharding import PartitionSpec as P

BLK = 32
MESH = pl.DeviceIdType.MESH
F32 = jnp.float32
BF16 = jnp.bfloat16
LOG2E = 1.4426950408889634


def dot(a, b, ca, cb):
    return lax.dot_general(a, b, (((ca,), (cb,)), ((), ())), preferred_element_type=F32)


def make_kernel(nz, ny, nx, nc, rows, width):
    nq = ny * nx
    nk = nz * nc
    seq = nq * nk * rows
    qn = nq * rows
    kn = nk * rows
    per = rows // BLK
    qw = nx * rows
    kw = nc * rows
    kb_count = kn // kw
    c2 = LOG2E / math.sqrt(width)
    grow = math.sqrt(rows * nq * nk * 0.5)
    side = grow / math.sqrt(width)

    def kernel(
        order_in, q_in, k_in, v_in, g_in, out_ref, dq_ref, dk_ref, dv_ref,
        order, qg, gg, kg, vg, qpos, kpos, scores, expo, dprob, dscore, stat, norm, stat_in,
        part, part_in, logs, logs_in, delta, delta_in, factor, mix, mix_in, dqs, dqs_in, own, core_out, core_in, z_out, z_in,
        results, out_sem, load_sem, q_s, q_r, g_s, g_r, k_s, k_r, kf_s, kf_r, v_s, v_r, vf_s, vf_r,
        st_s, st_r, pt_s, pt_r, lg_s, lg_r, de_s, de_r, mx_s, mx_r, dq_s, dq_r, co_s, co_r, zz_s, zz_r,
    ):
        z = lax.axis_index("qrow")
        col = lax.axis_index("kcol")
        y = col // (nx * nc)
        x = (col // nc) % nx
        c = col % nc

        def wrap(a, n):
            return a % n if isinstance(a, int) else jnp.where(a >= n, a - n, a)

        across = [wrap(x + k, nx) * nc + c for k in range(nx)]
        down = [wrap(y + r, ny) * (nx * nc) for r in range(ny)]
        peers = [down[j // nx] + across[j % nx] for j in range(nq)]
        layers = [wrap(z + d, nz) for d in range(nz)]
        other = col + 1 - 2 * c if nc == 2 else col
        sibling = (z, other)

        def z_peer(d):
            return (layers[d] if isinstance(d, int) else wrap(z + d, nz), col)

        def xy_peer(j):
            return (z, peers[j])

        def back_row(r):
            return wrap(ny - r, ny)

        def back_col(k):
            return wrap(nx - k, nx)

        def neg(j):
            return back_row(j // nx) * nx + back_col(j % nx)

        def copy(src, dst, send, recv, target):
            return pltpu.make_async_remote_copy(
                src_ref=src, dst_ref=dst, send_sem=send, recv_sem=recv,
                device_id=target, device_id_type=MESH,
            )

        def span(j):
            return pl.ds(j * rows if isinstance(j, int) else pl.multiple_of(j * rows, rows), rows)

        barrier = pltpu.get_barrier_semaphore()

        for target in [xy_peer(j) for j in range(1, nq)] + [z_peer(d) for d in range(1, nz)] + [sibling]:
            pl.semaphore_signal(barrier, inc=1, device_id=target, device_id_type=MESH)
        order_load = pltpu.make_async_copy(order_in, order, load_sem.at[4])
        order_load.start()
        loads = []
        for i, (src, dst) in enumerate(((k_in, kg), (q_in, qg), (v_in, vg), (g_in, gg))):
            load = pltpu.make_async_copy(src, dst.at[pl.ds(0, rows)], load_sem.at[i])
            load.start()
            loads.append(load)
        for load in loads:
            load.wait()
        pl.semaphore_wait(barrier, nq - 1 + nz - 1 + 1)

        def z_copy(buf, s, r, d):
            return copy(buf.at[pl.ds(0, rows)], buf.at[span(nc * d)], s.at[0], r.at[d], z_peer(nz - d))

        def f_copy(buf, s, r, d):
            return copy(buf.at[span(nc * d)], buf.at[span(nc * d + 1)], s.at[0], r.at[0], sibling)

        def xy_copy(buf, s, r, j):
            return copy(buf.at[pl.ds(0, rows)], buf.at[span(j)], s.at[0], r.at[0], xy_peer(neg(j)))

        def settle(like, sem):
            pltpu.make_async_copy(like, like, sem).wait()

        def each(lo, hi, what):
            for i in range(lo, hi):
                what(i)

        each(1, nz, lambda d: z_copy(kg, k_s, k_r, d).start())
        each(1, nq, lambda j: xy_copy(qg, q_s, q_r, j).start())
        f_copy(kg, kf_s, kf_r, 0).start()
        each(1, nz, lambda d: z_copy(vg, v_s, v_r, d).start())
        each(1, nq, lambda j: xy_copy(gg, g_s, g_r, j).start())
        f_copy(vg, vf_s, vf_r, 0).start()

        lane = lax.broadcasted_iota(jnp.int32, (8, rows), 1)
        low = lax.broadcasted_iota(jnp.int32, (BLK, 128), 0)

        def place_q(j):
            first = (z * (nq * nc) + peers[j]) * per
            block = jnp.zeros((8, rows), jnp.int32)
            for b in range(per):
                block = jnp.where(lane // BLK == b, order[first + b], block)
            qpos[:, span(j)] = block * BLK + lane % BLK

        def place_k(j):
            first = (layers[j // nc] * (nq * nc) + (col, other)[j % nc]) * per
            for b in range(per):
                kpos[pl.ds(j * rows + b * BLK, BLK), :] = order[first + b] * BLK + low

        order_load.wait()
        each(0, nq, place_q)
        each(0, nk, place_k)

        def pass_on(buf, s, r, fs, fr):
            for i in range(1, nz):
                d = (i + 1) // 2 if i % 2 == 1 else nz - i // 2
                z_copy(buf, s, r, d).wait_recv()
                f_copy(buf, fs, fr, d).start()

        pass_on(kg, k_s, k_r, kf_s, kf_r)
        settle(kg.at[pl.ds(0, nz * rows)], kf_r.at[0])
        settle(qg.at[pl.ds(rows, (nq - 1) * rows)], q_r.at[0])

        def up_copy(src, into, s, r, row, k):
            j = row * nx + k
            m = back_row(row) * nx + back_col(k)
            if isinstance(row, int):
                target = peers[j]
            else:
                target = wrap(y + row, ny) * (nx * nc) + (across[k] if isinstance(k, int) else wrap(x + k, nx) * nc + c)
            return copy(src(j), into.at[m], s.at[0], r.at[0], (z, target))

        def top_copy(row, k):
            return up_copy(lambda j: stat.at[:, span(j)], stat_in, st_s, st_r, row, k)

        def mean_copy(row, k):
            return up_copy(lambda j: part.at[:, span(j)], part_in, pt_s, pt_r, row, k)

        def mix_copy(row, k):
            return up_copy(lambda j: mix.at[j], mix_in, mx_s, mx_r, row, k)

        def dq_copy(row, k):
            return up_copy(lambda j: dqs.at[j], dqs_in, dq_s, dq_r, row, k)

        def back_copy(buf, into, s, r, j):
            return copy(buf, into.at[j], s.at[0], r.at[0], xy_peer(neg(j)))

        def log_copy(j):
            return back_copy(logs, logs_in, lg_s, lg_r, j)

        def delta_copy(j):
            return back_copy(delta, delta_in, de_s, de_r, j)

        def send_row(maker, row):
            @pl.when(row > 0)
            def _():
                maker(row, 0).start()

            for k in range(1, nx):
                maker(row, k).start()

        def scores_step(i, carry):
            @pl.when(i == ny - 1)
            def _():
                pass_on(vg, v_s, v_r, vf_s, vf_r)

            r = wrap(i + 1, ny)
            qs = pl.ds(pl.multiple_of(r * qw, qw), qw)
            q = qg[qs, :]
            qp = qpos[:, qs]
            top = None
            for kb in range(kb_count):
                ks = slice(kb * kw, (kb + 1) * kw)
                s = dot(kg[ks, :], q, 1, 1) * c2
                kp = jnp.concatenate([kpos[ks, :]] * (qw // 128), axis=1)
                s = jnp.where(kp <= qp[0:1], s, -1e30)
                scores[ks, :] = s
                high = jnp.max(s.reshape(kw // 8, 8, qw), axis=0)
                top = high if top is None else jnp.maximum(top, high)
            top = jnp.maximum(jnp.max(top, axis=0, keepdims=True), -1e29)
            total = jnp.zeros((8, qw), F32)
            for kb in range(kb_count):
                ks = slice(kb * kw, (kb + 1) * kw)
                e = jnp.exp2(scores[ks, :] - top)
                total = total + jnp.sum(e.reshape(kw // 8, 8, qw), axis=0)
                expo[ks, qs] = e.astype(BF16)
            stat[0:1, qs] = top
            stat[1:2, qs] = jnp.sum(total, axis=0, keepdims=True)
            send_row(top_copy, r)
            return carry

        lax.fori_loop(0, ny, scores_step, 0)
        stat_in[0] = stat[:, 0:rows]

        settle(vg.at[pl.ds(0, nz * rows)], vf_r.at[0])
        settle(gg.at[pl.ds(rows, (nq - 1) * rows)], g_r.at[0])

        def dprob_step(i, carry):
            r = wrap(i + 1, ny)
            qs = pl.ds(pl.multiple_of(r * qw, qw), qw)
            g = gg[qs, :]
            acc = jnp.zeros((8, qw), F32)
            for kb in range(kb_count):
                ks = slice(kb * kw, (kb + 1) * kw)
                d = dot(vg[ks, :], g, 1, 1)
                dprob[ks, qs] = d
                acc = acc + jnp.sum((expo[ks, qs].astype(F32) * d).reshape(kw // 8, 8, qw), axis=0)
            part[:, qs] = acc
            send_row(mean_copy, r)
            return carry

        lax.fori_loop(0, ny - 1, dprob_step, 0)

        settle(stat_in.at[pl.ds(1, nq - 1)], st_r.at[0])
        tops = stat_in[:, 0, :]
        best = jnp.max(tops, axis=0, keepdims=True)
        scale = jnp.exp2(tops - best)
        total = jnp.sum(stat_in[:, 1, :] * scale, axis=0, keepdims=True)
        factor[...] = scale / total
        logs[...] = jnp.broadcast_to(best + jnp.log(total) * LOG2E, (8, rows))
        each(1, nq, lambda j: log_copy(j).start())
        logs_in[0] = logs[...]

        lax.fori_loop(ny - 1, ny, dprob_step, 0)
        part_in[0] = part[:, 0:rows]

        def mix_step(i, carry):
            r = wrap(i + 1, ny)
            qs = pl.ds(pl.multiple_of(r * qw, qw), qw)
            o = dot(vg[...], expo[:, qs], 0, 0).astype(BF16)
            for k in range(nx):
                mix[r * nx + k] = o[:, k * rows:(k + 1) * rows]
            return carry

        lax.fori_loop(0, ny - 1, mix_step, 0)

        settle(part_in.at[pl.ds(1, nq - 1)], pt_r.at[0])
        acc = jnp.zeros((8, rows), F32)
        for j in range(nq):
            acc = acc + part_in[j] * factor[j:j + 1, :]
        delta[...] = jnp.broadcast_to(jnp.sum(acc, axis=0, keepdims=True), (8, rows))
        each(1, nq, lambda j: delta_copy(j).start())
        delta_in[0] = delta[...]

        lax.fori_loop(ny - 1, ny, mix_step, 0)

        settle(logs_in.at[pl.ds(1, nq - 1)], lg_r.at[0])

        def spread_logs(j):
            norm[0:1, span(j)] = jnp.exp2(stat[0:1, span(j)] - logs_in[j, 0:1, :])

        each(0, nq, spread_logs)

        def core_copy(n, d):
            return copy(core_out.at[n, d], core_in.at[n, d], co_s.at[0], co_r.at[n, d], sibling)

        def zz_copy(n, d):
            return copy(
                z_out.at[n, d], z_in.at[n, nz - d], zz_s.at[0], zz_r.at[n], z_peer(d)
            )

        lag = 2
        pairs = 2
        steps = nz // pairs

        def pair(i, e):
            return wrap((i + 1) * pairs, nz) + e

        def hand_on(n, i, value):
            for e in range(pairs):
                d = pair(i, e)
                own[n, d] = value[e * kw:e * kw + rows]
                core_out[n, d] = value[e * kw + rows:(e + 1) * kw].astype(BF16)
                core_copy(n, d).start()

        def to_owner(n, i):
            for e in range(pairs):
                d = pair(i, e)

                @pl.when(d > 0)
                def _():
                    core_copy(n, d).wait_recv()
                    z_out[n, d] = (own[n, d] + core_in[n, d].astype(F32)).astype(BF16)
                    zz_copy(n, d).start()

        def send_mix(j):
            mix_copy(j // nx, j - j // nx * nx).start()

        qb = 512

        def values_step(i, carry):
            for e in range(pairs):
                send_mix(i * pairs + e + 1)
            ks = pl.ds(pl.multiple_of(pair(i, 0) * kw, kw), pairs * kw)
            dv = jnp.zeros((pairs * kw, width), F32)
            for b in range(qn // qb):
                qs = slice(b * qb, (b + 1) * qb)
                p = expo[ks, qs].astype(F32) * norm[0:1, qs]
                dv = dv + dot(p.astype(BF16), gg[qs, :], 1, 0)
            hand_on(0, i, dv)

            @pl.when(i >= lag)
            def _():
                to_owner(0, i - lag)

            return carry

        lax.fori_loop(0, steps, values_step, 0)

        settle(delta_in.at[pl.ds(1, nq - 1)], de_r.at[0])

        def spread_delta(j):
            norm[1:2, span(j)] = delta_in[j, 0:1, :]

        each(0, nq, spread_delta)

        def keys_step(i, carry):
            for e in range(pairs):
                j = i * pairs + e + 1 + nz

                @pl.when(j < nq)
                def _():
                    send_mix(j)

            ks = pl.ds(pl.multiple_of(pair(i, 0) * kw, kw), pairs * kw)
            dk = jnp.zeros((pairs * kw, width), F32)
            for b in range(qn // qb):
                qs = slice(b * qb, (b + 1) * qb)
                p = expo[ks, qs].astype(F32) * norm[0:1, qs]
                ds = (p * (dprob[ks, qs] - norm[1:2, qs])).astype(BF16)
                dscore[ks, qs] = ds
                dk = dk + dot(ds, qg[qs, :], 1, 0)
            hand_on(1, i, dk)

            @pl.when(i < lag)
            def _():
                to_owner(0, i + steps - lag)

            @pl.when(i >= lag)
            def _():
                to_owner(1, i - lag)

            return carry

        lax.fori_loop(0, steps, keys_step, 0)

        def queries_step(i, carry):
            r = wrap(i + 1, ny)
            qs = pl.ds(pl.multiple_of(r * qw, qw), qw)
            o = dot(kg[...], dscore[:, qs], 0, 0)
            for k in range(nx):
                dqs[r * nx + k] = o[:, k * rows:(k + 1) * rows].astype(BF16)
            send_row(dq_copy, r)

            @pl.when(i < lag)
            def _():
                to_owner(1, i + steps - lag)

            return carry

        lax.fori_loop(0, ny, queries_step, 0)

        moves = []

        def leave(n, value, target):
            results[n] = value
            move = pltpu.make_async_copy(results.at[n], target, out_sem.at[n])
            move.start()
            moves.append(move)

        settle(mix_in.at[pl.ds(1, nq - 1)], mx_r.at[0])
        acc = mix[0].astype(F32) * factor[0:1, :]
        for j in range(1, nq):
            acc = acc + mix_in[j].astype(F32) * factor[j:j + 1, :]
        leave(0, acc.T, out_ref)

        for n, ref, by in ((0, dv_ref, grow), (1, dk_ref, side)):
            core_copy(n, 0).wait_recv()
            settle(z_in.at[n, pl.ds(1, nz - 1)], zz_r.at[n])
            acc = own[n, 0] + core_in[n, 0].astype(F32)
            for d in range(1, nz):
                acc = acc + z_in[n, d].astype(F32)
            leave(3 - n, acc * by, ref)

        settle(dqs_in.at[pl.ds(1, nq - 1)], dq_r.at[0])
        acc = dqs[0].astype(F32)
        for j in range(1, nq):
            acc = acc + dqs_in[j].astype(F32)
        leave(1, acc.T * side, dq_ref)

        for move in moves:
            move.wait()

        for like, sem in (
            (qg.at[pl.ds(0, (nq - 1) * rows)], q_s), (gg.at[pl.ds(0, (nq - 1) * rows)], g_s),
            (kg.at[pl.ds(0, (nz - 1) * rows)], k_s), (vg.at[pl.ds(0, (nz - 1) * rows)], v_s),
            (kg.at[pl.ds(0, nz * rows)], kf_s), (vg.at[pl.ds(0, nz * rows)], vf_s),
            (stat_in.at[pl.ds(1, nq - 1)], st_s), (part_in.at[pl.ds(1, nq - 1)], pt_s),
            (logs_in.at[pl.ds(1, nq - 1)], lg_s), (delta_in.at[pl.ds(1, nq - 1)], de_s),
            (mix.at[pl.ds(1, nq - 1)], mx_s), (dqs.at[pl.ds(1, nq - 1)], dq_s),
            (core_out, co_s), (z_out.at[:, pl.ds(1, nz - 1)], zz_s),
        ):
            settle(like, sem.at[0])

    dma = pltpu.SemaphoreType.DMA
    scratch = [
        pltpu.SMEM((seq // BLK,), jnp.int32),
        pltpu.VMEM((qn, width), BF16), pltpu.VMEM((qn, width), BF16),
        pltpu.VMEM((kn, width), BF16), pltpu.VMEM((kn, width), BF16),
        pltpu.VMEM((8, qn), jnp.int32), pltpu.VMEM((kn, 128), jnp.int32),
        pltpu.VMEM((kn, qw), F32), pltpu.VMEM((kn, qn), BF16),
        pltpu.VMEM((kn, qn), F32), pltpu.VMEM((kn, qn), BF16),
        pltpu.VMEM((8, qn), F32), pltpu.VMEM((8, qn), F32), pltpu.VMEM((nq, 8, rows), F32),
        pltpu.VMEM((8, qn), F32), pltpu.VMEM((nq, 8, rows), F32),
        pltpu.VMEM((8, rows), F32), pltpu.VMEM((nq, 8, rows), F32),
        pltpu.VMEM((8, rows), F32), pltpu.VMEM((nq, 8, rows), F32),
        pltpu.VMEM((nq, rows), F32),
        pltpu.VMEM((nq, width, rows), BF16), pltpu.VMEM((nq, width, rows), BF16),
        pltpu.VMEM((nq, width, rows), BF16), pltpu.VMEM((nq, width, rows), BF16),
        pltpu.VMEM((2, nz, rows, width), F32),
        pltpu.VMEM((2, nz, rows, width), BF16), pltpu.VMEM((2, nz, rows, width), BF16),
        pltpu.VMEM((2, nz, rows, width), BF16), pltpu.VMEM((2, nz, rows, width), BF16),
        pltpu.VMEM((4, rows, width), F32), dma((4,)),
        dma((5,)),
        dma((1,)), dma((1,)), dma((1,)), dma((1,)),
        dma((1,)), dma((nz,)), dma((1,)), dma((1,)),
        dma((1,)), dma((nz,)), dma((1,)), dma((1,)),
        dma((1,)), dma((1,)), dma((1,)), dma((1,)),
        dma((1,)), dma((1,)), dma((1,)), dma((1,)),
        dma((1,)), dma((1,)), dma((1,)), dma((1,)),
        dma((1,)), dma((2, nz)), dma((1,)), dma((2,)),
    ]
    vmem = pl.BlockSpec(memory_space=pltpu.VMEM)
    hbm = pl.BlockSpec(memory_space=pl.ANY)
    result = jax.ShapeDtypeStruct((rows, width), F32)
    return pl.pallas_call(
        kernel,
        name="banded_attention",
        out_shape=(result,) * 4,
        in_specs=[hbm] * 5,
        out_specs=(hbm,) * 4,
        scratch_shapes=scratch,
        compiler_params=pltpu.CompilerParams(
            collective_id=0, has_side_effects=True, vmem_limit_bytes=56 * 1024 * 1024
        ),
    )


def write_out(arrays, rows, width):
    def kernel(a, b, c, d, a_out, b_out, c_out, d_out):
        for source, target in ((a, a_out), (b, b_out), (c, c_out), (d, d_out)):
            target[...] = source[...]

    vmem = pl.BlockSpec(memory_space=pltpu.VMEM)
    return pl.pallas_call(
        kernel,
        name="write_out",
        out_shape=(jax.ShapeDtypeStruct((rows, width), F32),) * 4,
        in_specs=[vmem] * 4,
        out_specs=(vmem,) * 4,
        compiler_params=pltpu.CompilerParams(vmem_limit_bytes=56 * 1024 * 1024),
    )(*arrays)


def solution(mesh):
    nz = mesh.shape["qrow"]
    nc = 2
    nx = math.isqrt(mesh.shape["kcol"] // nc)
    ny = mesh.shape["kcol"] // (nc * nx)

    def body(queries, keys, values, cotangent, order):
        rows, width = queries.shape
        call = make_kernel(nz, ny, nx, nc, rows, width)
        return write_out(call(order, queries, keys, values, cotangent), rows, width)

    held = P(("qrow", "kcol"), None)
    return jax.shard_map(
        body,
        mesh=mesh,
        in_specs=(held, held, held, held, P()),
        out_specs=(held,) * 4,
        check_vma=False,
    )
```
